32 devices in a mesh: group: 2 (over y), attn: 4 (over z), expert: 4 (over x, core).
Axes of the slice: x: 2, y: 2, z: 4, core: 2. Of those that a mesh axis runs over, the one named last changes fastest.
Arguments:
- queries: bfloat16 [1024, 5120], P(('group', 'attn'), 'expert'), parts along dimension 0, may hold values from -30 to 30
- kv_cache: bfloat16 [2, 1024, 64, 1024], P(None, ('group', 'attn'), None, 'expert'), parts along dimension 1, may hold values from -30 to 30
- lengths: int32 [1024], P(('group', 'attn')), parts along dimension 0, may hold values from 2 to 64, as said below
- out_weight: bfloat16 [5120, 5120], P('expert', 'attn'), may hold values from -0.625 to 0.625
- residual: bfloat16 [1024, 5120], P(('group', 'expert'), 'attn'), parts along dimension 0, may hold values from -6 to 6
- norm_gain: bfloat16 [5120], P('attn'), may hold values from 0.099609375 to 1.8984375
- route_logit: float32 [1024], P(('group', 'expert')), parts along dimension 0, may hold values from -6 to 6
- routes: int32 [1024, 1], P(('group', 'expert')), parts along dimension 0, may hold values from 0 to 3; in each aligned block of 128 rows (0 to 127, 128 to 255, ...) at most 32 rows name the same one
- w_gate_up: bfloat16 [4, 2, 5120, 4096], P('expert', None, None, 'attn'), may hold values from -0.078125 to 0.078125
- w_down: bfloat16 [4, 4096, 5120], P('expert', None, 'attn'), may hold values from -0.09375 to 0.09375
Outputs:
- mixed: bfloat16 [1024, 5120], P(('group', 'expert'), 'attn'), parts along dimension 0
The draws below stay inside these ranges and needn't reach their ends.
There are 2 independent parts, one for each index of `group`. The reference program is written for one: setup_inputs(seed, part) draws one part's arguments, and reference() takes and returns one part's arrays. A program takes and returns all parts, laid end to end along the dimension named above; an argument that names none is the same for every part. Nothing has to cross between parts.
Inputs may be any that keep to these rules, and one draw needn't show every extreme that they name: `lengths`: request 0 has all 64 slots live. `routes`: within each aligned block of 128 requests no expert is named by more than 32 requests.
All inputs are finite; a program needn't handle non-finite values.
Results may differ from the reference program's by a relative error of at most 0.0049.
The reference program's roundings to bfloat16 on the way (of `probs`, `heads_out`, `normed`, `hidden_units` and `expert_out`) count: a program that leaves them out, or rounds other values in their place, can miss the bound.
Values may be sent and summed in bfloat16 or wider, within the bound.
A program may use at most 128 MiB of HBM per device.

```python
import math
import jax
import jax.numpy as jnp
import numpy as np
from jax import lax

D = 5120
HEADS = 40
KV_HEADS = 8
HD = 128
FF_EXP = 4096
LEN = 64
ROWS = 512
EXP_HELD = 4
MOE_ROWS = 128
CAP = 32


def draw_queries(key, part):
    key = jax.random.fold_in(key, 11)
    base = jnp.clip(jax.random.normal(key, (ROWS, KV_HEADS, HEADS // KV_HEADS, HD), jnp.float32), -6.0, 6.0)
    return base.reshape(ROWS, HEADS * HD).astype(jnp.bfloat16)


def draw_kv_cache(key, part):
    key = jax.random.fold_in(key, 12)
    base = jnp.clip(jax.random.normal(key, (2, ROWS, LEN, KV_HEADS, HD), jnp.float32), -6.0, 6.0)
    return base.reshape(2, ROWS, LEN, KV_HEADS * HD).astype(jnp.bfloat16)


def draw_lengths(key, part):
    key = jax.random.fold_in(key, 13)
    drawn = jax.random.randint(key, (ROWS,), 2, LEN + 1, dtype=jnp.int32)
    return drawn.at[0].set(LEN)


def steps_of(stream_key, shape, shards, low, high):
    level, own = 1.0, jax.random.fold_in(stream_key, 6)
    for position, blocks in shards:
        draws = jnp.exp(jax.random.uniform(jax.random.fold_in(own, position), (blocks,), jnp.float32, low / len(shards), high / len(shards)))
        level = level * jnp.repeat(draws, shape[position] // blocks).reshape([-1 if axis == position else 1 for axis in range(len(shape))])
    return level


def deal_out(rng, own, number, rows, count, top, reach, slope):
    sequence = jax.random.permutation(rng, count)
    packed, ordinary = load_shares(count, rows * top, reach, slope, True), load_shares(count, rows * top, reach, slope, False)
    places = jnp.arange(count)

    def named(sizes, offset_by):
        used = int((sizes > 0).sum())
        fixed = max(1, used // 4)
        moved = fixed + (places - fixed + offset_by * (used - fixed)) % max(1, count - fixed)
        return jnp.zeros((count,), jnp.int32).at[sequence[jnp.where(places < fixed, places, moved)]].set(jnp.asarray(sizes, jnp.int32))

    sizes = jnp.where(number % 4 == 0, named(packed, number // 4), named(ordinary, number - number // 4 - 1))
    mixed = jax.random.permutation(jax.random.fold_in(own, 3), count)
    source_of, taker = mixed[0:count // 2 * 2:2], mixed[1:count // 2 * 2:2]
    margin = jnp.minimum(sizes[source_of] - 1, reach - sizes[taker]) // 2
    margin = jnp.where((source_of == sequence[0]) | (taker == sequence[0]) | (sizes[taker] == 0), 0, jnp.maximum(margin, 0))
    moved = jax.random.randint(jax.random.fold_in(own, 4), (count // 2,), 0, 1 << 20) % (margin + 1)
    sizes = sizes.at[source_of].add(-moved).at[taker].add(moved)
    labels = jnp.searchsorted(jnp.cumsum(sizes), jnp.arange(rows * top), side="right").astype(jnp.int32)
    listing = labels.reshape(top, rows).T
    listing = listing[jax.random.permutation(jax.random.fold_in(own, 1), rows)]
    offset_by = jax.random.randint(jax.random.fold_in(own, 2), (rows, 1), 0, top)
    return jnp.take_along_axis(listing, (jnp.arange(top)[None, :] + offset_by) % top, axis=1)


def load_shares(number_of, total, bound, slope, full):
    portions = [(1 << 20) // math.isqrt(rank ** slope) + 1 for rank in range(1, number_of + 1)]
    largest = bound if full else min(bound, max(-(-total // number_of), total * portions[0] // sum(portions)))
    least = 1 if total - largest >= number_of - 1 else 0
    given, surplus = [largest] + [least] * (number_of - 1), total - largest - least * (number_of - 1)
    while surplus > 0:
        candidates = [i for i in range(1, number_of) if given[i] < largest] or [i for i in range(1, number_of) if given[i] < bound]
        whole, remaining = sum([portions[i] for i in candidates]), surplus
        for i in candidates:
            addition = min(bound - given[i], max(1, remaining * portions[i] // whole), surplus)
            given[i] = given[i] + addition
            surplus = surplus - addition
    return np.array(given)


def scatter_about(rng, shape, spread, most, shards=(), kind=jnp.bfloat16):
    entries = spread * jax.random.normal(rng, shape, jnp.float32)
    if shards:
        entries = entries * steps_of(rng, shape, shards, -0.22, 0.18)
    return jnp.clip(entries, -most, most).astype(kind)


def setup_inputs(seed: int = 0, part: int = 0) -> dict:
    seeds = jax.random.split(jax.random.key(seed), 11)
    own_keys = jax.random.split(jax.random.fold_in(seeds[10], part), 11)
    queries = draw_queries(jax.random.fold_in(jax.random.fold_in(seeds[10], part), 71), part)
    kv_cache = draw_kv_cache(jax.random.fold_in(jax.random.fold_in(seeds[10], part), 71), part)
    lengths = draw_lengths(jax.random.fold_in(jax.random.fold_in(seeds[10], part), 71), part)
    out_weight = scatter_about(seeds[3], (D, D), (D // 64) ** -0.5, 0.625, ((0, 4), (1, 4)))
    residual = scatter_about(own_keys[4], (ROWS, D), 1.0, 6.0, ((0, 4), (1, 4)))
    norm_gain = jnp.clip(1.0 + 0.18 * jax.random.normal(seeds[5], (D,), jnp.float32), 0.099609375, 1.8984375).astype(jnp.bfloat16)
    route_logit = scatter_about(own_keys[6], (ROWS,), 1.5, 6.0, ((0, 4),), jnp.float32)
    routes_keys = jax.random.split(jax.random.fold_in(own_keys[7], 1), ROWS // MOE_ROWS)
    routes_turns = jax.random.permutation(jax.random.fold_in(own_keys[7], 3), ROWS // MOE_ROWS)
    routes = jax.vmap(lambda own, number: deal_out(jax.random.fold_in(own_keys[7], 2), own, number, MOE_ROWS, EXP_HELD, 1, CAP, 2))(routes_keys, routes_turns).reshape((ROWS, 1))
    w_gate_up = scatter_about(seeds[8], (EXP_HELD, 2, D, FF_EXP), D ** -0.5, 0.078125, ((0, 4), (3, 4)))
    w_down = scatter_about(seeds[9], (EXP_HELD, FF_EXP, D), FF_EXP ** -0.5, 0.09375, ((0, 4), (2, 4)))
    return dict(queries=queries, kv_cache=kv_cache, lengths=lengths, out_weight=out_weight, residual=residual, norm_gain=norm_gain, route_logit=route_logit, routes=routes, w_gate_up=w_gate_up, w_down=w_down)


def attend_row(inputs):
    query_row, key_row, value_row, length = inputs
    group_size = HEADS // KV_HEADS
    query_heads = query_row.reshape(KV_HEADS, group_size, HD).astype(jnp.float32)
    key_heads = key_row.reshape(LEN, KV_HEADS, HD).astype(jnp.float32)
    value_heads = value_row.reshape(LEN, KV_HEADS, HD).astype(jnp.float32)
    scores = jnp.einsum('kgd,lkd->kgl', query_heads, key_heads) * (1.0 / math.sqrt(HD))
    live_mask = jnp.arange(LEN, dtype=jnp.int32) < length
    scores = jnp.where(live_mask[None, None, :], scores, -jnp.inf)
    row_peak = lax.optimization_barrier(jnp.max(scores, axis=-1, keepdims=True))
    expsum = jnp.exp(scores - row_peak)
    probs = (expsum / lax.optimization_barrier(jnp.sum(expsum, axis=-1, keepdims=True))).astype(jnp.bfloat16)
    heads_out = jnp.einsum('kgl,lkd->kgd', probs.astype(jnp.float32), value_heads)
    return heads_out.astype(jnp.bfloat16).reshape(D)

def reference(queries, kv_cache, lengths, out_weight, residual, norm_gain, route_logit, routes, w_gate_up, w_down):
    heads_out = lax.map(attend_row, (queries, kv_cache[0], kv_cache[1], lengths))
    projected = jnp.dot(heads_out, out_weight, preferred_element_type=jnp.float32)
    hidden_state = residual.astype(jnp.float32) + projected
    mean_sq = lax.optimization_barrier(jnp.mean(hidden_state * hidden_state, axis=1, keepdims=True))
    normed = (hidden_state * lax.rsqrt(mean_sq + 1e-05) * norm_gain.astype(jnp.float32)).astype(jnp.bfloat16)
    expert_out = jnp.zeros((ROWS, D), jnp.float32)
    for expert_id in range(EXP_HELD):
        gate_acc = jnp.dot(normed, w_gate_up[expert_id, 0], preferred_element_type=jnp.float32)
        up_acc = jnp.dot(normed, w_gate_up[expert_id, 1], preferred_element_type=jnp.float32)
        hidden_units = (jax.nn.silu(gate_acc) * up_acc).astype(jnp.bfloat16)
        result = jnp.dot(hidden_units, w_down[expert_id], preferred_element_type=jnp.float32).astype(jnp.bfloat16)
        expert_out = jnp.where(routes[:, :1] == expert_id, result.astype(jnp.float32), expert_out)
    gate_prob = jax.nn.sigmoid(route_logit.astype(jnp.float32))[:, None]
    return (hidden_state + gate_prob * expert_out).astype(jnp.bfloat16)
```

```python
import functools
import math

import jax
import jax.numpy as jnp
from jax import lax
from jax.experimental import pallas as pl
from jax.experimental.pallas import tpu as pltpu
from jax.sharding import PartitionSpec as P

HD = 128
GROUP_ROWS = 16
MESH = pl.DeviceIdType.MESH
F32 = jnp.float32
BF16 = jnp.bfloat16


def over_tiles(width, body):
    tile = 256 if width % 256 == 0 else width
    if tile == width:
        body(slice(None))
        return

    def step(j, carry):
        body(pl.ds(pl.multiple_of(j * tile, tile), tile))
        return carry

    lax.fori_loop(0, width // tile, step, 0)


class LineGather:
    def __init__(self, buf, send_sem, recv_sem, place, count, subs):
        self.buf, self.send_sem, self.recv_sem = buf, send_sem, recv_sem
        self.place, self.count, self.subs = place, count, subs

    def copy(self, block, sub, way):
        part = self.buf.at[block, sub]
        return pltpu.make_async_remote_copy(
            src_ref=part,
            dst_ref=part,
            send_sem=self.send_sem.at[way, block, sub],
            recv_sem=self.recv_sem.at[block, sub],
            device_id={"attn": self.place + (1 if way == 0 else -1)},
            device_id_type=MESH,
        )

    def can(self, way):
        return self.place < self.count - 1 if way == 0 else self.place > 0

    def forward(self, block, sub, way):
        @pl.when(self.can(way))
        def _():
            self.copy(block, sub, way).start()

    def send_own(self, sub):
        for way in range(2):
            self.forward(self.place, sub, way)

    def arrive(self, step, use):
        for way in range(2):
            block = self.place - step if way == 0 else self.place + step

            @pl.when(block >= 0 if way == 0 else block < self.count)
            def _():
                for sub in range(self.subs):
                    self.copy(block, sub, way).wait_recv()
                    self.forward(block, sub, way)
                use(block)

    def drain(self):
        def step(block, carry):
            for way in range(2):
                mine = block <= self.place if way == 0 else block >= self.place

                @pl.when(jnp.logical_and(self.can(way), mine))
                def _():
                    for sub in range(self.subs):
                        self.copy(block, sub, way).wait_send()

            return carry

        lax.fori_loop(0, self.count, step, 0)


def kernel(
    sizes,
    q_ref,
    kv_hbm,
    len_ref,
    wout_hbm,
    resid_ref,
    gain_ref,
    logit_ref,
    route_col_ref,
    route_row_ref,
    wgu_hbm,
    wd_hbm,
    out_ref,
    kv,
    wout,
    wgu,
    wd,
    ho,
    pbuf,
    mbuf,
    sbuf,
    xbuf,
    hid,
    qbuf,
    obuf,
    fbuf,
    scout,
    scin,
    gacc,
    hbuf,
    dacc,
    ebuf,
    rbuf,
    kv_sem,
    w_sem,
    ho_send,
    ho_recv,
    m_send,
    m_recv,
    x_send,
    x_recv,
    q_send,
    q_recv,
    o_send,
    o_recv,
    f_send,
    f_recv,
    s_send,
    s_recv,
    h_send,
    h_recv,
    r_send,
    r_recv,
):
    n_attn, n_exp = sizes
    n_chip = n_exp // 2
    z = lax.axis_index("attn")
    e = lax.axis_index("expert")
    x, c = e // 2, e % 2
    mate = e + 1 - 2 * c
    rows, q_cols = q_ref.shape
    span = kv.shape[2]
    kv_dev = kv.shape[3] // HD
    group_size = (q_cols // HD) // kv_dev
    moe_rows, cols = resid_ref.shape
    nsub = moe_rows // rows
    ff = wgu.shape[2]
    cap = moe_rows // 4
    slots = n_exp * cap
    ho_subs, h_subs = ho.shape[1], hbuf.shape[1]
    ff_sub = ff // h_subs
    groups = rows // GROUP_ROWS

    def kv_copy(g):
        part = pl.ds(g * GROUP_ROWS, GROUP_ROWS)
        return pltpu.make_async_copy(kv_hbm.at[:, part], kv.at[:, part], kv_sem.at[g])

    for g in range(groups):
        kv_copy(g).start()
    wout_copy = pltpu.make_async_copy(wout_hbm, wout, w_sem.at[0])
    wgu_copy = pltpu.make_async_copy(wgu_hbm.at[0], wgu, w_sem.at[1])
    wd_copy = pltpu.make_async_copy(wd_hbm.at[0], wd, w_sem.at[2])
    wout_copy.start()

    barrier = pltpu.get_barrier_semaphore()
    for d in range(1, n_attn):
        pl.semaphore_signal(
            barrier, inc=1, device_id={"attn": (z + d) % n_attn}, device_id_type=MESH
        )
    for d in range(1, n_exp):
        pl.semaphore_signal(
            barrier, inc=1, device_id={"expert": (e + d) % n_exp}, device_id_type=MESH
        )

    scale = 1.0 / math.sqrt(HD)
    wide = GROUP_ROWS * span
    sub_groups = groups // ho_subs

    def attend(sub, i):
        g = sub * sub_groups + i
        kv_copy(g).wait()
        part = pl.ds(pl.multiple_of(g * GROUP_ROWS, GROUP_ROWS), GROUP_ROWS)
        live = len_ref[part, :]
        first = lax.broadcasted_iota(jnp.int32, (GROUP_ROWS, wide), 0) * span
        slot = lax.broadcasted_iota(jnp.int32, (GROUP_ROWS, wide), 1) - first
        mask = jnp.logical_and(slot >= 0, slot < live)
        for k in range(kv_dev):
            lanes = slice(k * HD, (k + 1) * HD)
            heads = [k * group_size + h for h in range(group_size)]
            stacked = jnp.concatenate([q_ref[part, h * HD : (h + 1) * HD] for h in heads], axis=0)
            keys = kv[0, part, :, lanes].reshape(wide, HD)
            values = kv[1, part, :, lanes].reshape(wide, HD)
            s = lax.dot_general(
                stacked, keys, (((1,), (1,)), ((), ())), preferred_element_type=F32
            ) * scale
            s = jnp.where(mask[None], s.reshape(group_size, GROUP_ROWS, wide), -1e30)
            p = jnp.exp(s - jnp.max(s, axis=-1, keepdims=True))
            p = (p / jnp.sum(p, axis=-1, keepdims=True)).astype(BF16)
            o = jnp.dot(
                p.reshape(group_size * GROUP_ROWS, wide), values, preferred_element_type=F32
            ).astype(BF16)
            to = pl.ds(pl.multiple_of(i * GROUP_ROWS, GROUP_ROWS), GROUP_ROWS)
            for n, h in enumerate(heads):
                ho[z, sub, to, h * HD : (h + 1) * HD] = o[n * GROUP_ROWS : (n + 1) * GROUP_ROWS]

    ho_line = LineGather(ho, ho_send, ho_recv, z, n_attn, ho_subs)
    for sub in range(ho_subs):

        def attend_step(i, carry, sub=sub):
            attend(sub, i)
            return carry

        lax.fori_loop(0, sub_groups, attend_step, 0)
        if sub == 0:
            wgu_copy.start()
            wd_copy.start()
            pl.semaphore_wait(barrier, n_attn - 1 + n_exp - 1)
        ho_line.send_own(sub)

    def mate_copy(b):
        return pltpu.make_async_remote_copy(
            src_ref=pbuf.at[b],
            dst_ref=mbuf.at[b],
            send_sem=m_send.at[b],
            recv_sem=m_recv.at[b],
            device_id={"expert": mate},
            device_id_type=MESH,
        )

    def chip_copy(b):
        return pltpu.make_async_remote_copy(
            src_ref=sbuf.at[b],
            dst_ref=xbuf.at[x, b % nsub],
            send_sem=x_send.at[b],
            recv_sem=x_recv.at[x, b % nsub],
            device_id={"expert": (b // nsub) // 2 * 2 + c},
            device_id_type=MESH,
        )

    def chip_arrival(src, sub):
        return pltpu.make_async_remote_copy(
            src_ref=xbuf.at[src, sub],
            dst_ref=xbuf.at[src, sub],
            send_sem=x_send.at[0],
            recv_sem=x_recv.at[src, sub],
            device_id={"expert": src * 2 + c},
            device_id_type=MESH,
        )

    def project(b):
        block = ho[b].reshape(rows, q_cols)

        def tile(at):
            pbuf[b, :, at] = jnp.dot(block, wout[:, at], preferred_element_type=F32)

        over_tiles(cols, tile)

        @pl.when((b // nsub) % 2 != c)
        def _():
            mate_copy(b).start()

    def combine(b):
        @pl.when((b // nsub) % 2 == c)
        def _():
            mate_copy(b).wait_recv()

            @pl.when((b // nsub) // 2 != x)
            def _():
                sbuf[b] = (pbuf[b] + mbuf[b]).astype(BF16)
                chip_copy(b).start()

    wout_copy.wait()
    project(z)
    combine(z)

    def project_step(t, carry):
        ho_line.arrive(t, project)

        @pl.when(z - t >= 0)
        def _():
            combine(z - t)

        @pl.when(z + t < n_attn)
        def _():
            combine(z + t)

        return carry

    lax.fori_loop(1, n_attn, project_step, 0)

    route_row = route_row_ref[...]
    route_col = route_col_ref[...]
    at0 = lax.broadcasted_iota(jnp.int32, (moe_rows, moe_rows), 0)
    at1 = lax.broadcasted_iota(jnp.int32, (moe_rows, moe_rows), 1)
    same = route_col == route_row
    rank_row = jnp.sum(
        jnp.where(jnp.logical_and(same, at0 < at1), 1.0, 0.0), axis=0, keepdims=True
    ).astype(jnp.int32)
    rank_col = jnp.sum(
        jnp.where(jnp.logical_and(same, at1 < at0), 1.0, 0.0), axis=1, keepdims=True
    ).astype(jnp.int32)
    placed = (route_row * cap + rank_row) == lax.broadcasted_iota(
        jnp.int32, (slots, moe_rows), 0
    )
    placed_t = (route_col * cap + rank_col) == lax.broadcasted_iota(
        jnp.int32, (moe_rows, slots), 1
    )

    square_sum = None
    for sub in range(nsub):
        part = slice(sub * rows, (sub + 1) * rows)
        b = e * nsub + sub
        total = resid_ref[part, :].astype(F32) + (pbuf[b] + mbuf[b])
        for d in range(1, n_chip):
            src = (x + d) % n_chip
            chip_arrival(src, sub).wait_recv()
            total = total + xbuf[src, sub].astype(F32)
        hid[part, :] = total
    hidden = hid[...]
    square_sum = jnp.sum(hidden * hidden, axis=1, keepdims=True)
    square_row = jnp.sum(jnp.where(at0 == at1, square_sum, 0.0), axis=0, keepdims=True)
    qbuf[z] = jnp.broadcast_to(square_row, (8, moe_rows))

    def square_copy(d, src):
        return pltpu.make_async_remote_copy(
            src_ref=qbuf.at[src],
            dst_ref=qbuf.at[src],
            send_sem=q_send.at[d],
            recv_sem=q_recv.at[src],
            device_id={"attn": (z + d) % n_attn},
            device_id_type=MESH,
        )

    for d in range(1, n_attn):
        square_copy(d, z).start()

    scaled = (hidden * gain_ref[...].astype(F32)).astype(BF16)
    one_hot = jnp.where(placed, 1.0, 0.0).astype(BF16)
    obuf[...] = (
        jnp.dot(one_hot, scaled, preferred_element_type=F32).astype(BF16).reshape(n_exp, cap, cols)
    )

    def peer(d):
        to = (e + d) % n_exp
        return to, to // 2, to % 2

    def spread(src, dst, send_sem, recv_sem, to):
        return pltpu.make_async_remote_copy(
            src_ref=src,
            dst_ref=dst,
            send_sem=send_sem,
            recv_sem=recv_sem,
            device_id={"expert": to},
            device_id_type=MESH,
        )

    def dispatch_copy(d):
        to, to_x, _ = peer(d)
        rel = (x - to_x + n_chip) % n_chip
        return spread(
            obuf.at[to], fbuf.at[z, rel, c], o_send.at[d], o_recv.at[rel, c], to
        )

    def scale_copy(d):
        to, to_x, _ = peer(d)
        rel = (x - to_x + n_chip) % n_chip
        return spread(
            scout.at[to], scin.at[rel, c], s_send.at[d], s_recv.at[rel, c], to
        )

    def arrival(dst, sem):
        return spread(dst, dst, o_send.at[0], sem, mate)

    for d in range(1, n_exp):
        dispatch_copy(d).start()
    fbuf[z, 0, c] = obuf[e]
    f_line = LineGather(fbuf, f_send, f_recv, z, n_attn, n_chip)
    for rel in range(n_chip):
        if rel == 0:
            arrival(fbuf.at[z, 0, 1 - c], o_recv.at[0, 1 - c]).wait_recv()
        else:
            for core in range(2):
                arrival(fbuf.at[z, rel, core], o_recv.at[rel, core]).wait_recv()
        f_line.send_own(rel)

    wgu_copy.wait()
    gacc[...] = jnp.zeros_like(gacc)

    def expand(b):
        block = fbuf[b].reshape(slots, cols)
        depth = pl.ds(pl.multiple_of(b * cols, cols), cols)

        def tile(at):
            for i in range(2):
                gacc[i, :, at] += jnp.dot(block, wgu[i, depth, at], preferred_element_type=F32)

        over_tiles(ff, tile)

    expand(z)

    for d in range(1, n_attn):
        square_copy(0, (z + d) % n_attn).wait_recv()
    total_row = qbuf[0][:1]
    for a in range(1, n_attn):
        total_row = total_row + qbuf[a][:1]
    factor_row = lax.rsqrt(total_row / (cols * n_attn) + 1e-05)
    factor = jnp.sum(jnp.where(placed, factor_row, 0.0), axis=1, keepdims=True)
    scout[...] = jnp.broadcast_to(factor, (slots, HD)).reshape(n_exp, cap, HD)
    for d in range(1, n_exp):
        scale_copy(d).start()
    scin[0, c] = scout[e]

    def expand_step(t, carry):
        f_line.arrive(t, expand)
        return carry

    lax.fori_loop(1, n_attn, expand_step, 0)

    arrival(scin.at[0, 1 - c], s_recv.at[0, 1 - c]).wait_recv()
    for rel in range(1, n_chip):
        for core in range(2):
            arrival(scin.at[rel, core], s_recv.at[rel, core]).wait_recv()
    norm = scin[...].reshape(slots, HD)[:, :1]

    h_line = LineGather(hbuf, h_send, h_recv, z, n_attn, h_subs)
    for sub in range(h_subs):
        at = slice(sub * ff_sub, (sub + 1) * ff_sub)
        gate = gacc[0, :, at] * norm
        up = gacc[1, :, at] * norm
        hbuf[z, sub] = (gate / (1.0 + jnp.exp(-gate)) * up).astype(BF16)
        h_line.send_own(sub)

    wd_copy.wait()
    dacc[...] = jnp.zeros_like(dacc)

    def contract(b):
        def tile(at):
            total = dacc[:, at]
            for sub in range(h_subs):
                depth = pl.ds(pl.multiple_of(b * ff + sub * ff_sub, ff_sub), ff_sub)
                total = total + jnp.dot(hbuf[b, sub], wd[depth, at], preferred_element_type=F32)
            dacc[:, at] = total

        over_tiles(cols, tile)

    contract(z)

    def contract_step(t, carry):
        h_line.arrive(t, contract)
        return carry

    lax.fori_loop(1, n_attn, contract_step, 0)

    ebuf[...] = dacc[...].astype(BF16).reshape(n_chip, 2, cap, cols)

    def return_copy(d):
        to, to_x, to_c = peer(d)
        rel = (to_x - x + n_chip) % n_chip
        return spread(ebuf.at[rel, to_c], rbuf.at[e], r_send.at[d], r_recv.at[e], to)

    for d in range(1, n_exp):
        return_copy(d).start()
    rbuf[e] = ebuf[0, c]
    for d in range(1, n_exp):
        src = (e + d) % n_exp
        arrival(rbuf.at[src], r_recv.at[src]).wait_recv()
    one_hot_t = jnp.where(placed_t, 1.0, 0.0).astype(BF16)
    mixing = 1.0 / (1.0 + jnp.exp(-logit_ref[...]))
    combined = jnp.dot(one_hot_t, rbuf[...].reshape(slots, cols), preferred_element_type=F32)
    out_ref[...] = (hid[...] + mixing * combined).astype(BF16)

    ho_line.drain()
    f_line.drain()
    h_line.drain()

    def sums_left(b, carry):
        @pl.when((b // nsub) % 2 != c)
        def _():
            mate_copy(b).wait_send()

        @pl.when(jnp.logical_and((b // nsub) % 2 == c, (b // nsub) // 2 != x))
        def _():
            chip_copy(b).wait_send()

        return carry

    lax.fori_loop(0, n_attn, sums_left, 0)
    for d in range(1, n_attn):
        square_copy(d, z).wait_send()
    for d in range(1, n_exp):
        dispatch_copy(d).wait_send()
        scale_copy(d).wait_send()
        return_copy(d).wait_send()


def per_device(
    queries,
    kv_cache,
    lengths,
    out_weight,
    residual,
    norm_gain,
    route_logit,
    routes,
    w_gate_up,
    w_down,
):
    n_attn, n_exp = lax.axis_size("attn"), lax.axis_size("expert")
    n_chip = n_exp // 2
    rows, q_cols = queries.shape
    moe_rows, cols = residual.shape
    nsub = moe_rows // rows
    cap = moe_rows // 4
    slots = n_exp * cap
    ff = w_gate_up.shape[3]
    ho_subs, h_subs = 2, 2
    vmem = pl.BlockSpec(memory_space=pltpu.VMEM)
    hbm = pl.BlockSpec(memory_space=pl.ANY)
    dma = pltpu.SemaphoreType.DMA
    return pl.pallas_call(
        functools.partial(kernel, (n_attn, n_exp)),
        out_shape=jax.ShapeDtypeStruct((moe_rows, cols), BF16),
        in_specs=[vmem, hbm, vmem, hbm, vmem, vmem, vmem, vmem, vmem, hbm, hbm],
        out_specs=vmem,
        scratch_shapes=[
            pltpu.VMEM(kv_cache.shape, BF16),
            pltpu.VMEM(out_weight.shape, BF16),
            pltpu.VMEM(w_gate_up.shape[1:], BF16),
            pltpu.VMEM(w_down.shape[1:], BF16),
            pltpu.VMEM((n_attn, ho_subs, rows // ho_subs, q_cols), BF16),
            pltpu.VMEM((n_attn, rows, cols), F32),
            pltpu.VMEM((n_attn, rows, cols), F32),
            pltpu.VMEM((n_attn, rows, cols), BF16),
            pltpu.VMEM((n_chip, nsub, rows, cols), BF16),
            pltpu.VMEM((moe_rows, cols), F32),
            pltpu.VMEM((n_attn, 8, moe_rows), F32),
            pltpu.VMEM((n_exp, cap, cols), BF16),
            pltpu.VMEM((n_attn, n_chip, 2, cap, cols), BF16),
            pltpu.VMEM((n_exp, cap, HD), F32),
            pltpu.VMEM((n_chip, 2, cap, HD), F32),
            pltpu.VMEM((2, slots, ff), F32),
            pltpu.VMEM((n_attn, h_subs, slots, ff // h_subs), BF16),
            pltpu.VMEM((slots, cols), F32),
            pltpu.VMEM((n_chip, 2, cap, cols), BF16),
            pltpu.VMEM((n_exp, cap, cols), BF16),
            dma((rows // GROUP_ROWS,)),
            dma((3,)),
            dma((2, n_attn, ho_subs)),
            dma((n_attn, ho_subs)),
            dma((n_attn,)),
            dma((n_attn,)),
            dma((n_attn,)),
            dma((n_chip, nsub)),
            dma((n_attn,)),
            dma((n_attn,)),
            dma((n_exp,)),
            dma((n_chip, 2)),
            dma((2, n_attn, n_chip)),
            dma((n_attn, n_chip)),
            dma((n_exp,)),
            dma((n_chip, 2)),
            dma((2, n_attn, h_subs)),
            dma((n_attn, h_subs)),
            dma((n_exp,)),
            dma((n_exp,)),
        ],
        compiler_params=pltpu.CompilerParams(
            collective_id=0, has_side_effects=True, vmem_limit_bytes=63 * 1024 * 1024
        ),
    )(
        queries,
        kv_cache,
        lengths.reshape(rows, 1),
        out_weight,
        residual,
        norm_gain.reshape(1, cols),
        route_logit.reshape(moe_rows, 1),
        routes,
        routes.reshape(1, moe_rows),
        w_gate_up,
        w_down,
    )


def solution(mesh):
    return jax.shard_map(
        per_device,
        mesh=mesh,
        in_specs=(
            P(("group", "attn"), "expert"),
            P(None, ("group", "attn"), None, "expert"),
            P(("group", "attn")),
            P("expert", "attn"),
            P(("group", "expert"), "attn"),
            P("attn"),
            P(("group", "expert")),
            P(("group", "expert"), None),
            P("expert", None, None, "attn"),
            P("expert", None, "attn"),
        ),
        out_specs=P(("group", "expert"), "attn"),
        check_vma=False,
    )
```

```python
import functools
import math

import jax
import jax.numpy as jnp
from jax import lax
from jax.experimental import pallas as pl
from jax.experimental.pallas import tpu as pltpu
from jax.sharding import PartitionSpec as P

HD = 128
GROUP_ROWS = 16
MESH = pl.DeviceIdType.MESH
F32 = jnp.float32
BF16 = jnp.bfloat16


def over_tiles(width, body):
    tile = 256 if width % 256 == 0 else width
    if tile == width:
        body(slice(None))
        return

    def step(j, carry):
        body(pl.ds(pl.multiple_of(j * tile, tile), tile))
        return carry

    lax.fori_loop(0, width // tile, step, 0)


class LineGather:
    def __init__(self, buf, send_sem, recv_sem, place, count, subs):
        self.buf, self.send_sem, self.recv_sem = buf, send_sem, recv_sem
        self.place, self.count, self.subs = place, count, subs

    def copy(self, block, sub, way):
        part = self.buf.at[block, sub]
        return pltpu.make_async_remote_copy(
            src_ref=part,
            dst_ref=part,
            send_sem=self.send_sem.at[way, block, sub],
            recv_sem=self.recv_sem.at[block, sub],
            device_id={"attn": self.place + (1 if way == 0 else -1)},
            device_id_type=MESH,
        )

    def can(self, way):
        return self.place < self.count - 1 if way == 0 else self.place > 0

    def forward(self, block, sub, way):
        @pl.when(self.can(way))
        def _():
            self.copy(block, sub, way).start()

    def send_own(self, sub):
        for way in range(2):
            self.forward(self.place, sub, way)

    def arrive(self, step, use=None, use_part=None):
        def of_ways(act):
            for way in range(2):
                block = self.place - step if way == 0 else self.place + step

                @pl.when(block >= 0 if way == 0 else block < self.count)
                def _():
                    act(block, way)

        for sub in range(self.subs):

            def take(block, way, sub=sub):
                self.copy(block, sub, way).wait_recv()
                self.forward(block, sub, way)

            of_ways(take)
            if use_part is not None:
                of_ways(lambda block, way, sub=sub: use_part(block, sub))
        if use is not None:
            of_ways(lambda block, way: use(block))

    def drain(self):
        def step(block, carry):
            for way in range(2):
                mine = block <= self.place if way == 0 else block >= self.place

                @pl.when(jnp.logical_and(self.can(way), mine))
                def _():
                    for sub in range(self.subs):
                        self.copy(block, sub, way).wait_send()

            return carry

        lax.fori_loop(0, self.count, step, 0)


def kernel(
    sizes,
    q_ref,
    kv_hbm,
    len_ref,
    wout_hbm,
    resid_ref,
    gain_ref,
    logit_ref,
    route_row_ref,
    wgu_hbm,
    wd_hbm,
    out_ref,
    kv,
    wout,
    wgu,
    wd,
    ho,
    pbuf,
    mbuf,
    sbuf,
    xbuf,
    hid,
    qbuf,
    obuf,
    fbuf,
    scout,
    scin,
    gacc,
    hbuf,
    dacc,
    ebuf,
    rbuf,
    live_col,
    kv_sem,
    w_sem,
    ho_send,
    ho_recv,
    m_send,
    m_recv,
    x_send,
    x_recv,
    q_send,
    q_recv,
    o_send,
    o_recv,
    f_send,
    f_recv,
    s_send,
    s_recv,
    h_send,
    h_recv,
    r_send,
    r_recv,
):
    n_attn, n_exp = sizes
    n_chip = n_exp // 2
    z = lax.axis_index("attn")
    e = lax.axis_index("expert")
    x, c = e // 2, e % 2
    mate = e + 1 - 2 * c
    rows, q_cols = q_ref.shape
    span = kv.shape[2]
    kv_dev = kv.shape[3] // HD
    group_size = (q_cols // HD) // kv_dev
    moe_rows, cols = resid_ref.shape
    nsub = moe_rows // rows
    ff = wgu.shape[2]
    cap = moe_rows // 4
    slots = n_exp * cap
    ho_subs, h_subs = ho.shape[1], hbuf.shape[1]
    ff_sub = ff // h_subs
    groups = rows // GROUP_ROWS

    def kv_copy(g):
        part = pl.ds(g * GROUP_ROWS, GROUP_ROWS)
        return pltpu.make_async_copy(kv_hbm.at[:, part], kv.at[:, part], kv_sem.at[g])

    for g in range(groups):
        kv_copy(g).start()
    wout_copy = pltpu.make_async_copy(wout_hbm, wout, w_sem.at[0])
    wgu_copy = pltpu.make_async_copy(wgu_hbm.at[0], wgu, w_sem.at[1])
    wd_copy = pltpu.make_async_copy(wd_hbm.at[0], wd, w_sem.at[2])
    wout_copy.start()

    barrier = pltpu.get_barrier_semaphore()
    for d in range(1, n_attn):
        pl.semaphore_signal(
            barrier, inc=1, device_id={"attn": (z + d) % n_attn}, device_id_type=MESH
        )
    for d in range(1, n_exp):
        pl.semaphore_signal(
            barrier, inc=1, device_id={"expert": (e + d) % n_exp}, device_id_type=MESH
        )

    def column(row):
        side = row.shape[1]
        diagonal = lax.broadcasted_iota(jnp.int32, (side, side), 0) == lax.broadcasted_iota(
            jnp.int32, (side, side), 1
        )
        return jnp.sum(jnp.where(diagonal, row, 0.0), axis=1, keepdims=True)

    live_col[...] = jnp.broadcast_to(column(len_ref[...].astype(F32)), live_col.shape)

    scale = 1.0 / math.sqrt(HD)
    wide = GROUP_ROWS * span
    sub_groups = groups // ho_subs

    def attend(sub, i):
        g = sub * sub_groups + i
        kv_copy(g).wait()
        part = pl.ds(pl.multiple_of(g * GROUP_ROWS, GROUP_ROWS), GROUP_ROWS)
        live = live_col[part, :][:, :1].astype(jnp.int32)
        first = lax.broadcasted_iota(jnp.int32, (GROUP_ROWS, wide), 0) * span
        slot = lax.broadcasted_iota(jnp.int32, (GROUP_ROWS, wide), 1) - first
        mask = jnp.logical_and(slot >= 0, slot < live)
        for k in range(kv_dev):
            lanes = slice(k * HD, (k + 1) * HD)
            heads = [k * group_size + h for h in range(group_size)]
            stacked = jnp.concatenate([q_ref[part, h * HD : (h + 1) * HD] for h in heads], axis=0)
            keys = kv[0, part, :, lanes].reshape(wide, HD)
            values = kv[1, part, :, lanes].reshape(wide, HD)
            s = lax.dot_general(
                stacked, keys, (((1,), (1,)), ((), ())), preferred_element_type=F32
            ) * scale
            s = jnp.where(mask[None], s.reshape(group_size, GROUP_ROWS, wide), -1e30)
            p = jnp.exp(s - jnp.max(s, axis=-1, keepdims=True))
            p = (p / jnp.sum(p, axis=-1, keepdims=True)).astype(BF16)
            o = jnp.dot(
                p.reshape(group_size * GROUP_ROWS, wide), values, preferred_element_type=F32
            ).astype(BF16)
            to = pl.ds(pl.multiple_of(i * GROUP_ROWS, GROUP_ROWS), GROUP_ROWS)
            for n, h in enumerate(heads):
                ho[z, sub, to, h * HD : (h + 1) * HD] = o[n * GROUP_ROWS : (n + 1) * GROUP_ROWS]

    ho_line = LineGather(ho, ho_send, ho_recv, z, n_attn, ho_subs)
    for sub in range(ho_subs):

        def attend_step(i, carry, sub=sub):
            attend(sub, i)
            return carry

        lax.fori_loop(0, sub_groups, attend_step, 0)
        if sub == 0:
            wgu_copy.start()
            wd_copy.start()
            pl.semaphore_wait(barrier, n_attn - 1 + n_exp - 1)
        ho_line.send_own(sub)

    def mate_copy(b):
        return pltpu.make_async_remote_copy(
            src_ref=pbuf.at[b],
            dst_ref=mbuf.at[b],
            send_sem=m_send.at[b],
            recv_sem=m_recv.at[b],
            device_id={"expert": mate},
            device_id_type=MESH,
        )

    def chip_copy(b):
        return pltpu.make_async_remote_copy(
            src_ref=sbuf.at[b],
            dst_ref=xbuf.at[x, b % nsub],
            send_sem=x_send.at[b],
            recv_sem=x_recv.at[x, b % nsub],
            device_id={"expert": (b // nsub) // 2 * 2 + c},
            device_id_type=MESH,
        )

    def chip_arrival(src, sub):
        return pltpu.make_async_remote_copy(
            src_ref=xbuf.at[src, sub],
            dst_ref=xbuf.at[src, sub],
            send_sem=x_send.at[0],
            recv_sem=x_recv.at[src, sub],
            device_id={"expert": src * 2 + c},
            device_id_type=MESH,
        )

    def project(b):
        block = ho[b].reshape(rows, q_cols)

        def tile(at):
            pbuf[b, :, at] = jnp.dot(block, wout[:, at], preferred_element_type=F32)

        over_tiles(cols, tile)

        @pl.when((b // nsub) % 2 != c)
        def _():
            mate_copy(b).start()

    def combine(b):
        @pl.when((b // nsub) % 2 == c)
        def _():
            mate_copy(b).wait_recv()

            @pl.when((b // nsub) // 2 != x)
            def _():
                sbuf[b] = (pbuf[b] + mbuf[b]).astype(BF16)
                chip_copy(b).start()

    wout_copy.wait()
    project(z)
    combine(z)

    def project_step(t, carry):
        ho_line.arrive(t, project)

        @pl.when(z - t >= 0)
        def _():
            combine(z - t)

        @pl.when(z + t < n_attn)
        def _():
            combine(z + t)

        return carry

    lax.fori_loop(1, n_attn, project_step, 0)

    route_row = route_row_ref[...]
    route_col = column(route_row.astype(F32)).astype(jnp.int32)
    at0 = lax.broadcasted_iota(jnp.int32, (moe_rows, moe_rows), 0)
    at1 = lax.broadcasted_iota(jnp.int32, (moe_rows, moe_rows), 1)
    same = route_col == route_row
    rank_row = jnp.sum(
        jnp.where(jnp.logical_and(same, at0 < at1), 1.0, 0.0), axis=0, keepdims=True
    ).astype(jnp.int32)
    rank_col = jnp.sum(
        jnp.where(jnp.logical_and(same, at1 < at0), 1.0, 0.0), axis=1, keepdims=True
    ).astype(jnp.int32)
    placed = (route_row * cap + rank_row) == lax.broadcasted_iota(
        jnp.int32, (slots, moe_rows), 0
    )
    placed_t = (route_col * cap + rank_col) == lax.broadcasted_iota(
        jnp.int32, (moe_rows, slots), 1
    )

    square_sum = None
    for sub in range(nsub):
        part = slice(sub * rows, (sub + 1) * rows)
        b = e * nsub + sub
        total = resid_ref[part, :].astype(F32) + (pbuf[b] + mbuf[b])
        for d in range(1, n_chip):
            src = (x + d) % n_chip
            chip_arrival(src, sub).wait_recv()
            total = total + xbuf[src, sub].astype(F32)
        hid[part, :] = total
    hidden = hid[...]
    square_sum = jnp.sum(hidden * hidden, axis=1, keepdims=True)
    square_row = jnp.sum(jnp.where(at0 == at1, square_sum, 0.0), axis=0, keepdims=True)
    qbuf[z] = jnp.broadcast_to(square_row, (8, moe_rows))

    def square_copy(d, src):
        return pltpu.make_async_remote_copy(
            src_ref=qbuf.at[src],
            dst_ref=qbuf.at[src],
            send_sem=q_send.at[d],
            recv_sem=q_recv.at[src],
            device_id={"attn": (z + d) % n_attn},
            device_id_type=MESH,
        )

    for d in range(1, n_attn):
        square_copy(d, z).start()

    scaled = (hidden * gain_ref[...].astype(F32)).astype(BF16)
    one_hot = jnp.where(placed, 1.0, 0.0).astype(BF16)
    obuf[...] = (
        jnp.dot(one_hot, scaled, preferred_element_type=F32).astype(BF16).reshape(n_exp, cap, cols)
    )

    def peer(d):
        to = (e + d) % n_exp
        return to, to // 2, to % 2

    def spread(src, dst, send_sem, recv_sem, to):
        return pltpu.make_async_remote_copy(
            src_ref=src,
            dst_ref=dst,
            send_sem=send_sem,
            recv_sem=recv_sem,
            device_id={"expert": to},
            device_id_type=MESH,
        )

    def dispatch_copy(d):
        to, to_x, _ = peer(d)
        rel = (x - to_x + n_chip) % n_chip
        return spread(
            obuf.at[to], fbuf.at[z, rel, c], o_send.at[d], o_recv.at[rel, c], to
        )

    def scale_copy(d):
        to, to_x, _ = peer(d)
        rel = (x - to_x + n_chip) % n_chip
        return spread(
            scout.at[to], scin.at[rel, c], s_send.at[d], s_recv.at[rel, c], to
        )

    def arrival(dst, sem):
        return spread(dst, dst, o_send.at[0], sem, mate)

    for d in range(1, n_exp):
        dispatch_copy(d).start()
    fbuf[z, 0, c] = obuf[e]
    f_line = LineGather(fbuf, f_send, f_recv, z, n_attn, n_chip)
    for rel in range(n_chip):
        if rel == 0:
            arrival(fbuf.at[z, 0, 1 - c], o_recv.at[0, 1 - c]).wait_recv()
        else:
            for core in range(2):
                arrival(fbuf.at[z, rel, core], o_recv.at[rel, core]).wait_recv()
        f_line.send_own(rel)

    wgu_copy.wait()
    gacc[...] = jnp.zeros_like(gacc)

    def expand(b):
        block = fbuf[b].reshape(slots, cols)
        depth = pl.ds(pl.multiple_of(b * cols, cols), cols)

        def tile(at):
            for i in range(2):
                gacc[i, :, at] += jnp.dot(block, wgu[i, depth, at], preferred_element_type=F32)

        over_tiles(ff, tile)

    expand(z)

    for d in range(1, n_attn):
        square_copy(0, (z + d) % n_attn).wait_recv()
    total_row = qbuf[0][:1]
    for a in range(1, n_attn):
        total_row = total_row + qbuf[a][:1]
    factor_row = lax.rsqrt(total_row / (cols * n_attn) + 1e-05)
    factor = jnp.sum(jnp.where(placed, factor_row, 0.0), axis=1, keepdims=True)
    scout[...] = jnp.broadcast_to(factor, (slots, HD)).reshape(n_exp, cap, HD)
    for d in range(1, n_exp):
        scale_copy(d).start()
    scin[0, c] = scout[e]

    def expand_step(t, carry):
        f_line.arrive(t, expand)
        return carry

    lax.fori_loop(1, n_attn, expand_step, 0)

    arrival(scin.at[0, 1 - c], s_recv.at[0, 1 - c]).wait_recv()
    for rel in range(1, n_chip):
        for core in range(2):
            arrival(scin.at[rel, core], s_recv.at[rel, core]).wait_recv()
    norm = scin[...].reshape(slots, HD)[:, :1]

    h_line = LineGather(hbuf, h_send, h_recv, z, n_attn, h_subs)
    for sub in range(h_subs):
        at = slice(sub * ff_sub, (sub + 1) * ff_sub)
        gate = gacc[0, :, at] * norm
        up = gacc[1, :, at] * norm
        hbuf[z, sub] = (gate / (1.0 + jnp.exp(-gate)) * up).astype(BF16)
        h_line.send_own(sub)

    wd_copy.wait()
    dacc[...] = jnp.zeros_like(dacc)

    def contract(b, sub):
        depth = pl.ds(pl.multiple_of(b * ff + sub * ff_sub, ff_sub), ff_sub)

        def tile(at):
            dacc[:, at] += jnp.dot(hbuf[b, sub], wd[depth, at], preferred_element_type=F32)

        over_tiles(cols, tile)

    for sub in range(h_subs):
        contract(z, sub)

    def contract_step(t, carry):
        h_line.arrive(t, use_part=contract)
        return carry

    lax.fori_loop(1, n_attn, contract_step, 0)

    ebuf[...] = dacc[...].astype(BF16).reshape(n_chip, 2, cap, cols)

    def return_copy(d):
        to, to_x, to_c = peer(d)
        rel = (to_x - x + n_chip) % n_chip
        return spread(ebuf.at[rel, to_c], rbuf.at[e], r_send.at[d], r_recv.at[e], to)

    for d in range(1, n_exp):
        return_copy(d).start()
    rbuf[e] = ebuf[0, c]
    for d in range(1, n_exp):
        src = (e + d) % n_exp
        arrival(rbuf.at[src], r_recv.at[src]).wait_recv()
    one_hot_t = jnp.where(placed_t, 1.0, 0.0).astype(BF16)
    mixing = 1.0 / (1.0 + jnp.exp(-column(logit_ref[...])))
    combined = jnp.dot(one_hot_t, rbuf[...].reshape(slots, cols), preferred_element_type=F32)
    out_ref[...] = (hid[...] + mixing * combined).astype(BF16)

    ho_line.drain()
    f_line.drain()
    h_line.drain()

    def sums_left(b, carry):
        @pl.when((b // nsub) % 2 != c)
        def _():
            mate_copy(b).wait_send()

        @pl.when(jnp.logical_and((b // nsub) % 2 == c, (b // nsub) // 2 != x))
        def _():
            chip_copy(b).wait_send()

        return carry

    lax.fori_loop(0, n_attn, sums_left, 0)
    for d in range(1, n_attn):
        square_copy(d, z).wait_send()
    for d in range(1, n_exp):
        dispatch_copy(d).wait_send()
        scale_copy(d).wait_send()
        return_copy(d).wait_send()


def per_device(
    queries,
    kv_cache,
    lengths,
    out_weight,
    residual,
    norm_gain,
    route_logit,
    routes,
    w_gate_up,
    w_down,
):
    n_attn, n_exp = lax.axis_size("attn"), lax.axis_size("expert")
    n_chip = n_exp // 2
    rows, q_cols = queries.shape
    moe_rows, cols = residual.shape
    nsub = moe_rows // rows
    cap = moe_rows // 4
    slots = n_exp * cap
    ff = w_gate_up.shape[3]
    ho_subs, h_subs = 4, max(1, min(4, ff // 256))
    vmem = pl.BlockSpec(memory_space=pltpu.VMEM)
    hbm = pl.BlockSpec(memory_space=pl.ANY)
    dma = pltpu.SemaphoreType.DMA
    return pl.pallas_call(
        functools.partial(kernel, (n_attn, n_exp)),
        out_shape=jax.ShapeDtypeStruct((moe_rows, cols), BF16),
        in_specs=[vmem, hbm, vmem, hbm, vmem, vmem, vmem, vmem, hbm, hbm],
        out_specs=vmem,
        scratch_shapes=[
            pltpu.VMEM(kv_cache.shape, BF16),
            pltpu.VMEM(out_weight.shape, BF16),
            pltpu.VMEM(w_gate_up.shape[1:], BF16),
            pltpu.VMEM(w_down.shape[1:], BF16),
            pltpu.VMEM((n_attn, ho_subs, rows // ho_subs, q_cols), BF16),
            pltpu.VMEM((n_attn, rows, cols), F32),
            pltpu.VMEM((n_attn, rows, cols), F32),
            pltpu.VMEM((n_attn, rows, cols), BF16),
            pltpu.VMEM((n_chip, nsub, rows, cols), BF16),
            pltpu.VMEM((moe_rows, cols), F32),
            pltpu.VMEM((n_attn, 8, moe_rows), F32),
            pltpu.VMEM((n_exp, cap, cols), BF16),
            pltpu.VMEM((n_attn, n_chip, 2, cap, cols), BF16),
            pltpu.VMEM((n_exp, cap, HD), F32),
            pltpu.VMEM((n_chip, 2, cap, HD), F32),
            pltpu.VMEM((2, slots, ff), F32),
            pltpu.VMEM((n_attn, h_subs, slots, ff // h_subs), BF16),
            pltpu.VMEM((slots, cols), F32),
            pltpu.VMEM((n_chip, 2, cap, cols), BF16),
            pltpu.VMEM((n_exp, cap, cols), BF16),
            pltpu.VMEM((rows, HD), F32),
            dma((rows // GROUP_ROWS,)),
            dma((3,)),
            dma((2, n_attn, ho_subs)),
            dma((n_attn, ho_subs)),
            dma((n_attn,)),
            dma((n_attn,)),
            dma((n_attn,)),
            dma((n_chip, nsub)),
            dma((n_attn,)),
            dma((n_attn,)),
            dma((n_exp,)),
            dma((n_chip, 2)),
            dma((2, n_attn, n_chip)),
            dma((n_attn, n_chip)),
            dma((n_exp,)),
            dma((n_chip, 2)),
            dma((2, n_attn, h_subs)),
            dma((n_attn, h_subs)),
            dma((n_exp,)),
            dma((n_exp,)),
        ],
        compiler_params=pltpu.CompilerParams(
            collective_id=0, has_side_effects=True, vmem_limit_bytes=63 * 1024 * 1024
        ),
    )(
        queries,
        kv_cache,
        lengths.reshape(1, rows),
        out_weight,
        residual,
        norm_gain.reshape(1, cols),
        route_logit.reshape(1, moe_rows),
        routes.reshape(1, moe_rows),
        w_gate_up,
        w_down,
    )


def solution(mesh):
    return jax.shard_map(
        per_device,
        mesh=mesh,
        in_specs=(
            P(("group", "attn"), "expert"),
            P(None, ("group", "attn"), None, "expert"),
            P(("group", "attn")),
            P("expert", "attn"),
            P(("group", "expert"), "attn"),
            P("attn"),
            P(("group", "expert")),
            P(("group", "expert"), None),
            P("expert", None, None, "attn"),
            P("expert", None, "attn"),
        ),
        out_specs=P(("group", "expert"), "attn"),
        check_vma=False,
    )
```

```python
import functools
import math

import jax
import jax.numpy as jnp
from jax import lax
from jax.experimental import pallas as pl
from jax.experimental.pallas import tpu as pltpu
from jax.sharding import PartitionSpec as P

HD = 128
GROUP_ROWS = 16
MESH = pl.DeviceIdType.MESH
F32 = jnp.float32
BF16 = jnp.bfloat16


def over_tiles(width, body):
    tile = 256 if width % 256 == 0 else width
    if tile == width:
        body(slice(None))
        return

    def step(j, carry):
        body(pl.ds(pl.multiple_of(j * tile, tile), tile))
        return carry

    lax.fori_loop(0, width // tile, step, 0)


class LineGather:
    def __init__(self, buf, send_sem, recv_sem, place, count, subs):
        self.buf, self.send_sem, self.recv_sem = buf, send_sem, recv_sem
        self.place, self.count, self.subs = place, count, subs

    def copy(self, block, sub, way):
        part = self.buf.at[block, sub]
        return pltpu.make_async_remote_copy(
            src_ref=part,
            dst_ref=part,
            send_sem=self.send_sem.at[way, block, sub],
            recv_sem=self.recv_sem.at[block, sub],
            device_id={"attn": self.place + (1 if way == 0 else -1)},
            device_id_type=MESH,
        )

    def can(self, way):
        return self.place < self.count - 1 if way == 0 else self.place > 0

    def forward(self, block, sub, way):
        @pl.when(self.can(way))
        def _():
            self.copy(block, sub, way).start()

    def send_own(self, sub):
        for way in range(2):
            self.forward(self.place, sub, way)

    def arrive(self, step, use=None, use_part=None):
        def of_ways(act):
            for way in range(2):
                block = self.place - step if way == 0 else self.place + step

                @pl.when(block >= 0 if way == 0 else block < self.count)
                def _():
                    act(block, way)

        for sub in range(self.subs):

            def take(block, way, sub=sub):
                self.copy(block, sub, way).wait_recv()
                self.forward(block, sub, way)

            of_ways(take)
            if use_part is not None:
                of_ways(lambda block, way, sub=sub: use_part(block, sub))
        if use is not None:
            of_ways(lambda block, way: use(block))

    def drain(self):
        def step(block, carry):
            for way in range(2):
                mine = block <= self.place if way == 0 else block >= self.place

                @pl.when(jnp.logical_and(self.can(way), mine))
                def _():
                    for sub in range(self.subs):
                        self.copy(block, sub, way).wait_send()

            return carry

        lax.fori_loop(0, self.count, step, 0)


def kernel(
    sizes,
    q_ref,
    kv_hbm,
    len_ref,
    wout_hbm,
    resid_ref,
    gain_ref,
    logit_ref,
    route_row_ref,
    wgu_hbm,
    wd_hbm,
    out_ref,
    kv,
    wout,
    wgu,
    wd,
    ho,
    pbuf,
    mbuf,
    sbuf,
    xbuf,
    hid,
    qbuf,
    obuf,
    fbuf,
    scout,
    scin,
    gacc,
    hbuf,
    dacc,
    ebuf,
    rbuf,
    live_col,
    kv_sem,
    w_sem,
    ho_send,
    ho_recv,
    m_send,
    m_recv,
    x_send,
    x_recv,
    q_send,
    q_recv,
    o_send,
    o_recv,
    f_send,
    f_recv,
    s_send,
    s_recv,
    h_send,
    h_recv,
    r_send,
    r_recv,
):
    n_attn, n_exp = sizes
    n_chip = n_exp // 2
    z = lax.axis_index("attn")
    e = lax.axis_index("expert")
    x, c = e // 2, e % 2
    mate = e + 1 - 2 * c
    rows, q_cols = q_ref.shape
    span = kv.shape[2]
    kv_dev = kv.shape[3] // HD
    group_size = (q_cols // HD) // kv_dev
    moe_rows, cols = resid_ref.shape
    nsub = moe_rows // rows
    ff = wgu.shape[2]
    cap = moe_rows // 4
    slots = n_exp * cap
    ho_subs, h_subs = ho.shape[1], hbuf.shape[1]
    ff_sub = ff // h_subs
    groups = rows // GROUP_ROWS
    halves, width = pbuf.shape[1], pbuf.shape[3]

    def kv_copy(g):
        part = pl.ds(g * GROUP_ROWS, GROUP_ROWS)
        return pltpu.make_async_copy(kv_hbm.at[:, part], kv.at[:, part], kv_sem.at[g])

    for g in range(groups):
        kv_copy(g).start()
    wout_copy = pltpu.make_async_copy(wout_hbm, wout, w_sem.at[0])
    wgu_copy = pltpu.make_async_copy(wgu_hbm.at[0], wgu, w_sem.at[1])
    wd_copy = pltpu.make_async_copy(wd_hbm.at[0], wd, w_sem.at[2])
    wout_copy.start()

    barrier = pltpu.get_barrier_semaphore()
    for d in range(1, n_attn):
        pl.semaphore_signal(
            barrier, inc=1, device_id={"attn": (z + d) % n_attn}, device_id_type=MESH
        )
    for d in range(1, n_exp):
        pl.semaphore_signal(
            barrier, inc=1, device_id={"expert": (e + d) % n_exp}, device_id_type=MESH
        )

    def column(row):
        side = row.shape[1]
        diagonal = lax.broadcasted_iota(jnp.int32, (side, side), 0) == lax.broadcasted_iota(
            jnp.int32, (side, side), 1
        )
        return jnp.sum(jnp.where(diagonal, row, 0.0), axis=1, keepdims=True)

    live_col[...] = jnp.broadcast_to(column(len_ref[...].astype(F32)), live_col.shape)

    scale = 1.0 / math.sqrt(HD)
    wide = GROUP_ROWS * span
    sub_groups = groups // ho_subs

    def attend(sub, i):
        g = sub * sub_groups + i
        kv_copy(g).wait()
        part = pl.ds(pl.multiple_of(g * GROUP_ROWS, GROUP_ROWS), GROUP_ROWS)
        live = live_col[part, :][:, :1].astype(jnp.int32)
        first = lax.broadcasted_iota(jnp.int32, (GROUP_ROWS, wide), 0) * span
        slot = lax.broadcasted_iota(jnp.int32, (GROUP_ROWS, wide), 1) - first
        mask = jnp.logical_and(slot >= 0, slot < live)
        for k in range(kv_dev):
            lanes = slice(k * HD, (k + 1) * HD)
            heads = [k * group_size + h for h in range(group_size)]
            stacked = jnp.concatenate([q_ref[part, h * HD : (h + 1) * HD] for h in heads], axis=0)
            keys = kv[0, part, :, lanes].reshape(wide, HD)
            values = kv[1, part, :, lanes].reshape(wide, HD)
            s = lax.dot_general(
                stacked, keys, (((1,), (1,)), ((), ())), preferred_element_type=F32
            ) * scale
            s = jnp.where(mask[None], s.reshape(group_size, GROUP_ROWS, wide), -1e30)
            p = jnp.exp(s - jnp.max(s, axis=-1, keepdims=True))
            p = (p / jnp.sum(p, axis=-1, keepdims=True)).astype(BF16)
            o = jnp.dot(
                p.reshape(group_size * GROUP_ROWS, wide), values, preferred_element_type=F32
            ).astype(BF16)
            to = pl.ds(pl.multiple_of(i * GROUP_ROWS, GROUP_ROWS), GROUP_ROWS)
            for n, h in enumerate(heads):
                ho[z, sub, to, h * HD : (h + 1) * HD] = o[n * GROUP_ROWS : (n + 1) * GROUP_ROWS]

    ho_line = LineGather(ho, ho_send, ho_recv, z, n_attn, ho_subs)
    for sub in range(ho_subs):

        def attend_step(i, carry, sub=sub):
            attend(sub, i)
            return carry

        lax.fori_loop(0, sub_groups, attend_step, 0)
        if sub == 0:
            wgu_copy.start()
            wd_copy.start()
            pl.semaphore_wait(barrier, n_attn - 1 + n_exp - 1)
        ho_line.send_own(sub)

    def mate_copy(b, half):
        return pltpu.make_async_remote_copy(
            src_ref=pbuf.at[b, half],
            dst_ref=mbuf.at[b, half],
            send_sem=m_send.at[b, half],
            recv_sem=m_recv.at[b, half],
            device_id={"expert": mate},
            device_id_type=MESH,
        )

    def chip_copy(b, half):
        return pltpu.make_async_remote_copy(
            src_ref=sbuf.at[b, half],
            dst_ref=xbuf.at[x, b % nsub, half],
            send_sem=x_send.at[b, half],
            recv_sem=x_recv.at[x, b % nsub, half],
            device_id={"expert": (b // nsub) // 2 * 2 + c},
            device_id_type=MESH,
        )

    def chip_arrival(src, sub, half):
        return pltpu.make_async_remote_copy(
            src_ref=xbuf.at[src, sub, half],
            dst_ref=xbuf.at[src, sub, half],
            send_sem=x_send.at[0, 0],
            recv_sem=x_recv.at[src, sub, half],
            device_id={"expert": src * 2 + c},
            device_id_type=MESH,
        )

    def project(b):
        block = ho[b].reshape(rows, q_cols)
        for half in range(halves):
            at = slice(half * width, (half + 1) * width)
            pbuf[b, half] = jnp.dot(block, wout[:, at], preferred_element_type=F32)

            @pl.when((b // nsub) % 2 != c)
            def _():
                mate_copy(b, half).start()

    def combine(b):
        @pl.when((b // nsub) % 2 == c)
        def _():
            for half in range(halves):
                mate_copy(b, half).wait_recv()

                @pl.when((b // nsub) // 2 != x)
                def _():
                    sbuf[b, half] = (pbuf[b, half] + mbuf[b, half]).astype(BF16)
                    chip_copy(b, half).start()

    wout_copy.wait()
    project(z)
    combine(z)

    def project_step(t, carry):
        ho_line.arrive(t, project)

        @pl.when(z - t >= 0)
        def _():
            combine(z - t)

        @pl.when(z + t < n_attn)
        def _():
            combine(z + t)

        return carry

    lax.fori_loop(1, n_attn, project_step, 0)

    route_row = route_row_ref[...]
    route_col = column(route_row.astype(F32)).astype(jnp.int32)
    at0 = lax.broadcasted_iota(jnp.int32, (moe_rows, moe_rows), 0)
    at1 = lax.broadcasted_iota(jnp.int32, (moe_rows, moe_rows), 1)
    same = route_col == route_row
    rank_row = jnp.sum(
        jnp.where(jnp.logical_and(same, at0 < at1), 1.0, 0.0), axis=0, keepdims=True
    ).astype(jnp.int32)
    rank_col = jnp.sum(
        jnp.where(jnp.logical_and(same, at1 < at0), 1.0, 0.0), axis=1, keepdims=True
    ).astype(jnp.int32)
    placed = (route_row * cap + rank_row) == lax.broadcasted_iota(
        jnp.int32, (slots, moe_rows), 0
    )
    placed_t = (route_col * cap + rank_col) == lax.broadcasted_iota(
        jnp.int32, (moe_rows, slots), 1
    )

    square_sum = None
    for sub in range(nsub):
        part = slice(sub * rows, (sub + 1) * rows)
        b = e * nsub + sub
        for half in range(halves):
            at = slice(half * width, (half + 1) * width)
            total = resid_ref[part, at].astype(F32) + (pbuf[b, half] + mbuf[b, half])
            for d in range(1, n_chip):
                src = (x + d) % n_chip
                chip_arrival(src, sub, half).wait_recv()
                total = total + xbuf[src, sub, half].astype(F32)
            hid[part, at] = total
    hidden = hid[...]
    square_sum = jnp.sum(hidden * hidden, axis=1, keepdims=True)
    square_row = jnp.sum(jnp.where(at0 == at1, square_sum, 0.0), axis=0, keepdims=True)
    qbuf[z] = jnp.broadcast_to(square_row, (8, moe_rows))

    def square_copy(d, src):
        return pltpu.make_async_remote_copy(
            src_ref=qbuf.at[src],
            dst_ref=qbuf.at[src],
            send_sem=q_send.at[d],
            recv_sem=q_recv.at[src],
            device_id={"attn": (z + d) % n_attn},
            device_id_type=MESH,
        )

    for d in range(1, n_attn):
        square_copy(d, z).start()

    scaled = (hidden * gain_ref[...].astype(F32)).astype(BF16)
    one_hot = jnp.where(placed, 1.0, 0.0).astype(BF16)
    obuf[...] = (
        jnp.dot(one_hot, scaled, preferred_element_type=F32).astype(BF16).reshape(n_exp, cap, cols)
    )

    def peer(d):
        to = (e + d) % n_exp
        return to, to // 2, to % 2

    def spread(src, dst, send_sem, recv_sem, to):
        return pltpu.make_async_remote_copy(
            src_ref=src,
            dst_ref=dst,
            send_sem=send_sem,
            recv_sem=recv_sem,
            device_id={"expert": to},
            device_id_type=MESH,
        )

    def dispatch_copy(d):
        to, to_x, _ = peer(d)
        rel = (x - to_x + n_chip) % n_chip
        return spread(
            obuf.at[to], fbuf.at[z, rel, c], o_send.at[d], o_recv.at[rel, c], to
        )

    def scale_copy(d):
        to, to_x, _ = peer(d)
        rel = (x - to_x + n_chip) % n_chip
        return spread(
            scout.at[to], scin.at[rel, c], s_send.at[d], s_recv.at[rel, c], to
        )

    def arrival(dst, sem):
        return spread(dst, dst, o_send.at[0], sem, mate)

    for d in range(1, n_exp):
        dispatch_copy(d).start()
    fbuf[z, 0, c] = obuf[e]
    f_line = LineGather(fbuf, f_send, f_recv, z, n_attn, n_chip)
    for rel in range(n_chip):
        if rel == 0:
            arrival(fbuf.at[z, 0, 1 - c], o_recv.at[0, 1 - c]).wait_recv()
        else:
            for core in range(2):
                arrival(fbuf.at[z, rel, core], o_recv.at[rel, core]).wait_recv()
        f_line.send_own(rel)

    wgu_copy.wait()
    gacc[...] = jnp.zeros_like(gacc)

    def expand(b):
        block = fbuf[b].reshape(slots, cols)
        depth = pl.ds(pl.multiple_of(b * cols, cols), cols)

        def tile(at):
            for i in range(2):
                gacc[i, :, at] += jnp.dot(block, wgu[i, depth, at], preferred_element_type=F32)

        over_tiles(ff, tile)

    expand(z)

    for d in range(1, n_attn):
        square_copy(0, (z + d) % n_attn).wait_recv()
    total_row = qbuf[0][:1]
    for a in range(1, n_attn):
        total_row = total_row + qbuf[a][:1]
    factor_row = lax.rsqrt(total_row / (cols * n_attn) + 1e-05)
    factor = jnp.sum(jnp.where(placed, factor_row, 0.0), axis=1, keepdims=True)
    scout[...] = jnp.broadcast_to(factor, (slots, HD)).reshape(n_exp, cap, HD)
    for d in range(1, n_exp):
        scale_copy(d).start()
    scin[0, c] = scout[e]

    def expand_step(t, carry):
        f_line.arrive(t, expand)
        return carry

    lax.fori_loop(1, n_attn, expand_step, 0)

    arrival(scin.at[0, 1 - c], s_recv.at[0, 1 - c]).wait_recv()
    for rel in range(1, n_chip):
        for core in range(2):
            arrival(scin.at[rel, core], s_recv.at[rel, core]).wait_recv()
    norm = scin[...].reshape(slots, HD)[:, :1]

    h_line = LineGather(hbuf, h_send, h_recv, z, n_attn, h_subs)
    for sub in range(h_subs):
        at = slice(sub * ff_sub, (sub + 1) * ff_sub)
        gate = gacc[0, :, at] * norm
        up = gacc[1, :, at] * norm
        hbuf[z, sub] = (gate / (1.0 + jnp.exp(-gate)) * up).astype(BF16)
        h_line.send_own(sub)

    wd_copy.wait()
    dacc[...] = jnp.zeros_like(dacc)

    def contract(b, sub):
        depth = pl.ds(pl.multiple_of(b * ff + sub * ff_sub, ff_sub), ff_sub)

        def tile(at):
            dacc[:, at] += jnp.dot(hbuf[b, sub], wd[depth, at], preferred_element_type=F32)

        over_tiles(cols, tile)

    for sub in range(h_subs):
        contract(z, sub)

    def contract_step(t, carry):
        h_line.arrive(t, use_part=contract)
        return carry

    lax.fori_loop(1, n_attn, contract_step, 0)

    ebuf[...] = dacc[...].astype(BF16).reshape(n_chip, 2, cap, cols)

    def return_copy(d):
        to, to_x, to_c = peer(d)
        rel = (to_x - x + n_chip) % n_chip
        return spread(ebuf.at[rel, to_c], rbuf.at[e], r_send.at[d], r_recv.at[e], to)

    for d in range(1, n_exp):
        return_copy(d).start()
    rbuf[e] = ebuf[0, c]
    for d in range(1, n_exp):
        src = (e + d) % n_exp
        arrival(rbuf.at[src], r_recv.at[src]).wait_recv()
    one_hot_t = jnp.where(placed_t, 1.0, 0.0).astype(BF16)
    mixing = 1.0 / (1.0 + jnp.exp(-column(logit_ref[...])))
    combined = jnp.dot(one_hot_t, rbuf[...].reshape(slots, cols), preferred_element_type=F32)
    out_ref[...] = (hid[...] + mixing * combined).astype(BF16)

    ho_line.drain()
    f_line.drain()
    h_line.drain()

    def sums_left(b, carry):
        @pl.when((b // nsub) % 2 != c)
        def _():
            for half in range(halves):
                mate_copy(b, half).wait_send()

        @pl.when(jnp.logical_and((b // nsub) % 2 == c, (b // nsub) // 2 != x))
        def _():
            for half in range(halves):
                chip_copy(b, half).wait_send()

        return carry

    lax.fori_loop(0, n_attn, sums_left, 0)
    for d in range(1, n_attn):
        square_copy(d, z).wait_send()
    for d in range(1, n_exp):
        dispatch_copy(d).wait_send()
        scale_copy(d).wait_send()
        return_copy(d).wait_send()


def per_device(
    queries,
    kv_cache,
    lengths,
    out_weight,
    residual,
    norm_gain,
    route_logit,
    routes,
    w_gate_up,
    w_down,
):
    n_attn, n_exp = lax.axis_size("attn"), lax.axis_size("expert")
    n_chip = n_exp // 2
    rows, q_cols = queries.shape
    moe_rows, cols = residual.shape
    nsub = moe_rows // rows
    cap = moe_rows // 4
    slots = n_exp * cap
    ff = w_gate_up.shape[3]
    halves = 2 if cols % (2 * HD) == 0 else 1
    width = cols // halves
    ho_subs, h_subs = 4, max(1, min(4, ff // 256))
    vmem = pl.BlockSpec(memory_space=pltpu.VMEM)
    hbm = pl.BlockSpec(memory_space=pl.ANY)
    dma = pltpu.SemaphoreType.DMA
    return pl.pallas_call(
        functools.partial(kernel, (n_attn, n_exp)),
        out_shape=jax.ShapeDtypeStruct((moe_rows, cols), BF16),
        in_specs=[vmem, hbm, vmem, hbm, vmem, vmem, vmem, vmem, hbm, hbm],
        out_specs=vmem,
        scratch_shapes=[
            pltpu.VMEM(kv_cache.shape, BF16),
            pltpu.VMEM(out_weight.shape, BF16),
            pltpu.VMEM(w_gate_up.shape[1:], BF16),
            pltpu.VMEM(w_down.shape[1:], BF16),
            pltpu.VMEM((n_attn, ho_subs, rows // ho_subs, q_cols), BF16),
            pltpu.VMEM((n_attn, halves, rows, width), F32),
            pltpu.VMEM((n_attn, halves, rows, width), F32),
            pltpu.VMEM((n_attn, halves, rows, width), BF16),
            pltpu.VMEM((n_chip, nsub, halves, rows, width), BF16),
            pltpu.VMEM((moe_rows, cols), F32),
            pltpu.VMEM((n_attn, 8, moe_rows), F32),
            pltpu.VMEM((n_exp, cap, cols), BF16),
            pltpu.VMEM((n_attn, n_chip, 2, cap, cols), BF16),
            pltpu.VMEM((n_exp, cap, HD), F32),
            pltpu.VMEM((n_chip, 2, cap, HD), F32),
            pltpu.VMEM((2, slots, ff), F32),
            pltpu.VMEM((n_attn, h_subs, slots, ff // h_subs), BF16),
            pltpu.VMEM((slots, cols), F32),
            pltpu.VMEM((n_chip, 2, cap, cols), BF16),
            pltpu.VMEM((n_exp, cap, cols), BF16),
            pltpu.VMEM((rows, HD), F32),
            dma((rows // GROUP_ROWS,)),
            dma((3,)),
            dma((2, n_attn, ho_subs)),
            dma((n_attn, ho_subs)),
            dma((n_attn, halves)),
            dma((n_attn, halves)),
            dma((n_attn, halves)),
            dma((n_chip, nsub, halves)),
            dma((n_attn,)),
            dma((n_attn,)),
            dma((n_exp,)),
            dma((n_chip, 2)),
            dma((2, n_attn, n_chip)),
            dma((n_attn, n_chip)),
            dma((n_exp,)),
            dma((n_chip, 2)),
            dma((2, n_attn, h_subs)),
            dma((n_attn, h_subs)),
            dma((n_exp,)),
            dma((n_exp,)),
        ],
        compiler_params=pltpu.CompilerParams(
            collective_id=0, has_side_effects=True, vmem_limit_bytes=63 * 1024 * 1024
        ),
    )(
        queries,
        kv_cache,
        lengths.reshape(1, rows),
        out_weight,
        residual,
        norm_gain.reshape(1, cols),
        route_logit.reshape(1, moe_rows),
        routes.reshape(1, moe_rows),
        w_gate_up,
        w_down,
    )


def solution(mesh):
    return jax.shard_map(
        per_device,
        mesh=mesh,
        in_specs=(
            P(("group", "attn"), "expert"),
            P(None, ("group", "attn"), None, "expert"),
            P(("group", "attn")),
            P("expert", "attn"),
            P(("group", "expert"), "attn"),
            P("attn"),
            P(("group", "expert")),
            P(("group", "expert"), None),
            P("expert", None, None, "attn"),
            P("expert", None, "attn"),
        ),
        out_specs=P(("group", "expert"), "attn"),
        check_vma=False,
    )
```
